32 devices in a mesh: parts: 2 (over y), row: 4 (over z), col: 4 (over x, core).
Axes of the slice: x: 2, y: 2, z: 4, core: 2. Of those that a mesh axis runs over, the one named last changes fastest.
Arguments:
- normed: bfloat16 [2048, 6144], P(('parts', 'row'), 'col'), parts along dimension 0, may hold values from -6 to 6
- cotangent: bfloat16 [2048, 6144], P(('parts', 'row'), 'col'), parts along dimension 0, may hold values from -6 to 6
- w_up: bfloat16 [6144, 24576], P('col', 'row'), may hold values from -0.078125 to 0.078125
- w_down: bfloat16 [24576, 6144], P('row', 'col'), may hold values from -0.0390625 to 0.0390625
- sign_in_up: int32 [6144, 64], P('col'), may hold values from 0 to 1
- sign_out_up: int32 [24576, 64], P('row'), may hold values from 0 to 1
- sign_in_down: int32 [24576, 64], P('row'), may hold values from 0 to 1
- sign_out_down: int32 [6144, 64], P('col'), may hold values from 0 to 1
- patch_order: int32 [2048], P('parts'), parts along dimension 0, may hold values from 0 to 1023, each once
Outputs:
- sketch_up: float32 [8, 4096], P('parts', ('row', 'col')), parts along dimension 0
- sketch_down: float32 [8, 4096], P('parts', ('row', 'col')), parts along dimension 0
The draws below stay inside these ranges and needn't reach their ends.
There are 2 independent parts, one for each index of `parts`. The reference program is written for one: setup_inputs(seed, part) draws one part's arguments, and reference() takes and returns one part's arrays. A program takes and returns all parts, laid end to end along the dimension named above; an argument that names none is the same for every part. Nothing has to cross between parts.
All inputs are finite; a program needn't handle non-finite values.
Results may differ from the reference program's by a relative error of at most 0.015.
Values may be sent and summed in bfloat16 or wider, within the bound.
No kernel may reach another device: no remote copies, remote signals or barrier semaphores. Data moves between devices by JAX's collectives and lax.ppermute only.
A program may use at most 192 MiB of HBM per device.

```python
import jax
import jax.numpy as jnp
from jax import lax

D = 6144
FF = 24576
K = 64
PATCHES = 256
IMAGES = 4
TOKENS = 1024
N_COL = 4


def plant(values, own_key, least, high):
    longest = values.shape.index(max(values.shape))
    spots = []
    for shift in (0, 1):
        where = [jax.random.randint(jax.random.fold_in(own_key, axis), (), 0, length) for axis, length in enumerate(values.shape)]
        where[longest] = (where[longest] + shift) % values.shape[longest]
        spots.append(tuple(where))
    return values.at[spots[0]].set(least).at[spots[1]].set(high)


def block_levels(stream_key, shape, cuts, low, top_value):
    gain = 1.0
    for dim, blocks in cuts:
        steps = jax.random.uniform(jax.random.fold_in(jax.random.fold_in(stream_key, 6), dim), (blocks,), jnp.float32, low / len(cuts), top_value / len(cuts))
        gain = gain * jnp.repeat(jnp.exp(steps), shape[dim] // blocks).reshape((-1,) + (1,) * (len(shape) - 1 - dim))
    return gain


def noise(rng, shape, spread, reach, cuts=(), held_as=jnp.bfloat16):
    values = jax.random.normal(rng, shape, jnp.float32) * spread
    if len(cuts) > 0:
        values = block_levels(rng, shape, cuts, -0.22, 0.18) * values
    return jnp.clip(values, min=-reach, max=reach).astype(held_as)


def setup_inputs(seed: int = 0, part: int = 0) -> dict:
    seeds = jax.random.split(jax.random.key(seed), 10)
    part_keys = jax.random.split(jax.random.fold_in(seeds[9], part), 10)
    return {
        "normed": noise(part_keys[0], (TOKENS, D), 1.0, 6.0, ((0, 4), (1, 4))),
        "cotangent": noise(part_keys[1], (TOKENS, D), 1.0, 6.0, ((0, 4), (1, 4))),
        "w_up": noise(seeds[2], (D, FF), D ** -0.5, 0.078125, ((0, 4), (1, 4))),
        "w_down": noise(seeds[3], (FF, D), FF ** -0.5, 0.0390625, ((0, 4), (1, 4))),
        "sign_in_up": plant(jax.random.randint(seeds[4], (D, K), 0, 2), jax.random.fold_in(seeds[4], 1), 0, 1).astype(jnp.int32),
        "sign_out_up": plant(jax.random.randint(seeds[5], (FF, K), 0, 2), jax.random.fold_in(seeds[5], 1), 0, 1).astype(jnp.int32),
        "sign_in_down": plant(jax.random.randint(seeds[6], (FF, K), 0, 2), jax.random.fold_in(seeds[6], 1), 0, 1).astype(jnp.int32),
        "sign_out_down": plant(jax.random.randint(seeds[7], (D, K), 0, 2), jax.random.fold_in(seeds[7], 1), 0, 1).astype(jnp.int32),
        "patch_order": jax.random.permutation(part_keys[8], TOKENS).astype(jnp.int32),
    }


def rounded_blocks(left_side, right_side):
    block_width = left_side.shape[1] // N_COL

    def add_block(block_index, running):
        first_row = jnp.asarray(block_index * block_width).astype(jnp.int32)
        product_piece = jnp.dot(lax.dynamic_slice_in_dim(left_side, first_row, block_width, 1),
                                lax.dynamic_slice_in_dim(right_side, first_row, block_width, 0),
                                preferred_element_type=jnp.float32)
        return running + lax.optimization_barrier(product_piece.astype(jnp.bfloat16)).astype(jnp.float32)

    initial = jnp.zeros((left_side.shape[0], right_side.shape[1]), jnp.float32)
    return lax.fori_loop(0, N_COL, add_block, initial)


def reference(normed, cotangent, w_up, w_down, sign_in_up, sign_out_up, sign_in_down, sign_out_down, patch_order):
    signs_a = (2 * sign_in_up - 1).astype(jnp.bfloat16)
    signs_b = (2 * sign_out_up - 1).astype(jnp.bfloat16)
    signs_c = (2 * sign_in_down - 1).astype(jnp.bfloat16)
    signs_e = (2 * sign_out_down - 1).astype(jnp.bfloat16)
    hidden_pre = rounded_blocks(normed, w_up)
    hidden_back = rounded_blocks(cotangent, jnp.transpose(w_down))
    proj_up = rounded_blocks(normed, signs_a)
    proj_down = rounded_blocks(cotangent, signs_e)
    normal_cdf = 0.5 * (1.0 + lax.erf(hidden_pre * 0.7071067811865476))
    normal_pdf = jnp.exp(-0.5 * hidden_pre * hidden_pre) * 0.3989422804014327
    activation = (hidden_pre * normal_cdf).astype(jnp.bfloat16)
    dgrad = (hidden_back * (normal_cdf + hidden_pre * normal_pdf)).astype(jnp.bfloat16)
    side_up = jnp.dot(dgrad, signs_b, preferred_element_type=jnp.float32)
    side_down = jnp.dot(activation, signs_c, preferred_element_type=jnp.float32)
    images = patch_order // PATCHES
    member_table = (images[None, :] == jnp.arange(IMAGES, dtype=jnp.int32)[:, None]).astype(jnp.float32)
    sketch_scale = 1.0 / (float(D) * float(FF) * float(PATCHES)) ** 0.5
    sketch_up = jnp.einsum("it,tk,tl->ikl", member_table, proj_up, side_up, precision=lax.Precision.HIGHEST)
    sketch_down = jnp.einsum("it,tk,tl->ikl", member_table, side_down, proj_down, precision=lax.Precision.HIGHEST)
    return (sketch_up.reshape(IMAGES, -1) * sketch_scale, sketch_down.reshape(IMAGES, -1) * sketch_scale)
```

```python
import functools

import jax
import jax.numpy as jnp
from jax import lax
from jax.experimental import pallas as pl
from jax.experimental.pallas import tpu as pltpu
from jax.sharding import PartitionSpec as P

D = 6144
FF = 24576
PATCHES = 256
IMAGES = 4
SCALE = 1.0 / (float(D) * float(FF) * float(PATCHES)) ** 0.5
BF16 = jnp.bfloat16
F32 = jnp.float32


def gelu_terms(pre):
    cdf = 0.5 * (1.0 + lax.erf(pre * 0.7071067811865476))
    pdf = jnp.exp(-0.5 * pre * pre) * 0.3989422804014327
    return pre * cdf, cdf + pre * pdf


def sign_matrix(bits):
    return (2 * bits - 1).astype(BF16)


def members(patch_order):
    images = patch_order // PATCHES
    return (images[None, :] == jnp.arange(IMAGES, dtype=jnp.int32)[:, None]).astype(F32)


def gathered(normed, cotangent, w_up, w_down, sign_in_up, sign_out_up, sign_in_down, sign_out_down, patch_order):
    k = sign_in_up.shape[1]
    x = lax.all_gather(normed, "row", axis=0, tiled=True)
    g = lax.all_gather(cotangent, "row", axis=0, tiled=True)
    up = jnp.dot(x, w_up, preferred_element_type=F32)
    down = lax.dot_general(g, w_down, (((1,), (1,)), ((), ())), preferred_element_type=F32)
    proj = jnp.concatenate(
        [
            jnp.dot(x, sign_matrix(sign_in_up), preferred_element_type=F32),
            jnp.dot(g, sign_matrix(sign_out_down), preferred_element_type=F32),
        ],
        axis=1,
    )
    pre = lax.psum_scatter(up.astype(BF16), "col", scatter_dimension=1, tiled=True).astype(F32)
    back = lax.psum_scatter(down.astype(BF16), "col", scatter_dimension=1, tiled=True).astype(F32)
    proj = lax.psum(proj.astype(BF16), "col").astype(F32)
    units = pre.shape[1]
    first = lax.axis_index("col") * units
    sb = sign_matrix(lax.dynamic_slice_in_dim(sign_out_up, first, units, 0))
    sc = sign_matrix(lax.dynamic_slice_in_dim(sign_in_down, first, units, 0))
    act, slope = gelu_terms(pre)
    side_up = jnp.dot((back * slope).astype(BF16), sb, preferred_element_type=F32)
    side_down = jnp.dot(act.astype(BF16), sc, preferred_element_type=F32)
    table = members(patch_order)
    high = lax.Precision.HIGHEST
    up = jnp.einsum("it,tk,tl->ikl", table, proj[:, :k], side_up, precision=high)
    down = jnp.einsum("it,tk,tl->ikl", table, side_down, proj[:, k:], precision=high)
    return tuple(
        lax.psum_scatter(t.reshape(IMAGES, -1) * SCALE, ("row", "col"), scatter_dimension=1, tiled=True)
        for t in (up, down)
    )


def columns(w_ref, contract, first, size):
    return w_ref.at[:, pl.ds(first, size)] if contract == 0 else w_ref.at[pl.ds(first, size), :]


def tiles_of(units):
    cuts, at = [], 0
    for part in (1, 2, 3, 3, 2, 1):
        size = units * part // 12
        cuts.append((at, size))
        at += size
    return cuts if units % 1536 == 0 else [(0, units)]


def partial_kernel(contract, tiles, pick_ref, order_ref, *refs):
    n = 6 if contract == 0 else 2
    ins, w_ref, refs = refs[:n], refs[n], refs[n + 1 :]
    send_refs, (fwd_ref, keep_ref), refs = refs[:PIECES], refs[PIECES : PIECES + 2], refs[PIECES + 2 :]
    if contract == 0:
        p_ref, rows, y_ref, w_v, row_sem, w_sem, out_sem, other, bits, other_sem, bits_sem = refs
    else:
        rows, y_ref, w_v, row_sem, w_sem, out_sem = refs
    quarter = rows.shape[0] // 4
    piece = 2 * quarter // PIECES
    parts = [(n * piece, piece, ref) for n, ref in enumerate(send_refs)]
    parts += [(2 * quarter, quarter, fwd_ref), (3 * quarter, quarter, keep_ref)]

    def row_copies(source, target, sem):
        return [
            pltpu.make_async_copy(
                source.at[pl.ds(pl.multiple_of(order_ref[j] * quarter, quarter), quarter), :],
                target.at[pl.ds(j * quarter, quarter), :],
                sem.at[j],
            )
            for j in range(4)
        ]

    for choice in (0, 1):

        @pl.when(pick_ref[0] == choice)
        def _():
            for copy in row_copies(ins[choice], rows, row_sem):
                copy.start()

    loads = [
        pltpu.make_async_copy(columns(w_ref, contract, *t), columns(w_v, contract, *t), w_sem.at[j])
        for j, t in enumerate(tiles)
    ]
    for copy in loads[:AHEAD]:
        copy.start()
    for copy in row_copies(ins[0], rows, row_sem):
        copy.wait()
    if contract == 0:
        for choice in (0, 1):

            @pl.when(pick_ref[0] == choice)
            def _():
                for copy in row_copies(ins[2 + choice], other, other_sem):
                    copy.start()

        bit_copies = [pltpu.make_async_copy(ins[4 + n], bits.at[n], bits_sem.at[n]) for n in range(2)]
        for copy in bit_copies:
            copy.start()
    outs = []
    for j, (first_unit, size) in enumerate(tiles):
        loads[j].wait()
        if j + AHEAD < len(tiles):
            loads[j + AHEAD].start()
        at = pl.ds(first_unit, size)
        y_ref[:, at] = lax.dot_general(
            rows[...],
            columns(w_v, contract, first_unit, size)[...],
            (((1,), (contract,)), ((), ())),
            preferred_element_type=F32,
        ).astype(BF16)
        for n, (first, count, out) in enumerate(parts):
            copy = pltpu.make_async_copy(y_ref.at[pl.ds(first, count), at], out.at[:, at], out_sem.at[n, j])
            copy.start()
            outs.append(copy)
    if contract == 0:
        for copy in row_copies(ins[2], other, other_sem) + bit_copies:
            copy.wait()
        p_ref[...] = jnp.concatenate(
            [
                lax.dot_general(
                    left[...], (2 * bits[n] - 1).astype(F32).astype(BF16), ACROSS_DIMS, preferred_element_type=F32
                )
                for n, left in enumerate((rows, other))
            ],
            axis=1,
        ).astype(BF16)
    for copy in outs:
        copy.wait()


ACROSS_DIMS = (((1,), (1,)), ((), ()))
COST = 4.8e9
ECOST = 4.8e9
AHEAD = 3
PIECES = 4


def in_hbm(*arrays):
    return [pltpu.with_memory_space_constraint(a, pltpu.HBM) for a in arrays]


def partial_product(pick, order, x, w, contract, g=None, bits=None):
    tokens, depth = x[0].shape
    units = w.shape[1 - contract]
    tiles = tiles_of(units)
    quarter = tokens // 4
    anywhere = pl.BlockSpec(memory_space=pl.ANY)
    scalars = pl.BlockSpec(memory_space=pltpu.SMEM)
    vmem = pl.BlockSpec(memory_space=pltpu.VMEM)
    ins, outs, scratch = [*x], [], []
    if g is not None:
        ins += [*g, *bits]
        outs = [jax.ShapeDtypeStruct((tokens, 2 * bits[0].shape[0]), BF16)]
        scratch = [
            pltpu.VMEM((tokens, depth), BF16),
            pltpu.VMEM((2, *bits[0].shape), bits[0].dtype),
            pltpu.SemaphoreType.DMA((4,)),
            pltpu.SemaphoreType.DMA((2,)),
        ]
    ins = in_hbm(*ins, w)
    return pl.pallas_call(
        functools.partial(partial_kernel, contract, tiles),
        in_specs=[scalars, scalars] + [anywhere] * len(ins),
        out_specs=[anywhere] * (PIECES + 2) + [vmem] * len(outs),
        out_shape=[pltpu.HBM((2 * quarter // PIECES, units), BF16)] * PIECES
        + [pltpu.HBM((quarter, units), BF16)] * 2
        + outs,
        scratch_shapes=[
            pltpu.VMEM((tokens, depth), BF16),
            pltpu.VMEM((tokens, units), BF16),
            pltpu.VMEM(w.shape, BF16),
            pltpu.SemaphoreType.DMA((4,)),
            pltpu.SemaphoreType.DMA((len(tiles),)),
            pltpu.SemaphoreType.DMA((PIECES + 2, len(tiles))),
        ]
        + scratch,
        compiler_params=pltpu.CompilerParams(vmem_limit_bytes=36 * 2**20),
        cost_estimate=pl.CostEstimate(flops=int(COST), bytes_accessed=1000, transcendentals=0),
    )(pick, order, *ins)


def add_kernel(a_ref, *refs):
    terms, (out_ref, slots, sems) = refs[:-3], refs[-3:]
    piece = terms[0].shape[0]
    copies = [pltpu.make_async_copy(a_ref, slots.at[0], sems.at[0])]
    for n, ref in enumerate(terms):
        copies.append(pltpu.make_async_copy(ref, slots.at[1, pl.ds(n * piece, piece), :], sems.at[1 + n]))
    for copy in copies:
        copy.start()
    for copy in copies:
        copy.wait()
    out_ref[...] = (slots[0].astype(F32) + slots[1].astype(F32)).astype(BF16)


def add_rows(a, b):
    return pl.pallas_call(
        add_kernel,
        in_specs=[pl.BlockSpec(memory_space=pl.ANY)] * (1 + len(b)),
        out_specs=pl.BlockSpec(memory_space=pltpu.VMEM),
        out_shape=jax.ShapeDtypeStruct(a.shape, BF16),
        scratch_shapes=[pltpu.VMEM((2, *a.shape), BF16), pltpu.SemaphoreType.DMA((1 + len(b),))],
        compiler_params=pltpu.CompilerParams(vmem_limit_bytes=16 * 2**20),
        cost_estimate=pl.CostEstimate(flops=1000, bytes_accessed=1000, transcendentals=0),
    )(*in_hbm(a, *b))


def signs_kernel(b_ref, c_ref, sb_ref, sc_ref):
    sb_ref[...] = (2 * b_ref[...] - 1).astype(F32).astype(BF16)
    sc_ref[...] = (2 * c_ref[...] - 1).astype(F32).astype(BF16)


def both_signs(after, b, c):
    vmem = pl.BlockSpec(memory_space=pltpu.VMEM)
    k, units = b.shape
    tile = 1536 if units % 1536 == 0 else units
    block = pl.BlockSpec((k, tile), lambda j: (0, j))
    return pl.pallas_call(
        lambda after_ref, *refs: signs_kernel(*refs),
        grid=(units // tile,),
        in_specs=[pl.BlockSpec(memory_space=pl.ANY), block, block],
        out_specs=[block] * 2,
        out_shape=[jax.ShapeDtypeStruct(b.shape, BF16)] * 2,
        cost_estimate=pl.CostEstimate(flops=1000, bytes_accessed=1000, transcendentals=0),
    )(after, b, c)


def gathered_terms(refs, slots, sems):
    piece = refs[2].shape[0]
    copies = [
        pltpu.make_async_copy(refs[0], slots.at[0], sems.at[0]),
        pltpu.make_async_copy(refs[1], slots.at[1], sems.at[1]),
    ]
    for n, ref in enumerate(refs[2:]):
        copies.append(pltpu.make_async_copy(ref, slots.at[2, pl.ds(n * piece, piece), :], sems.at[2 + n]))
    for copy in copies:
        copy.start()
    return copies


def total(slots, at):
    return slots[0, :, at].astype(F32) + slots[1, :, at].astype(F32) + slots[2, :, at].astype(F32)


def chunks_of(units):
    chunk = 1024 if units % 1024 == 0 else units
    return [pl.ds(j * chunk, chunk) for j in range(units // chunk)]


def act_kernel(n, *refs):
    terms, (sc, down_ref, slope_ref, slots, sems) = refs[: n + 2], refs[n + 2 :]
    for copy in gathered_terms(terms, slots, sems):
        copy.wait()
    side = jnp.zeros(down_ref.shape, F32)
    for at in chunks_of(slope_ref.shape[1]):
        act, slope = gelu_terms(total(slots, at))
        side += lax.dot_general(act.astype(BF16), sc[:, at], ACROSS_DIMS, preferred_element_type=F32)
        slope_ref[:, at] = slope
    down_ref[...] = side


def back_kernel(n, *refs):
    terms, (slope_ref, sb, up_ref, slots, sems) = refs[: n + 2], refs[n + 2 :]
    for copy in gathered_terms(terms, slots, sems):
        copy.wait()
    side = jnp.zeros(up_ref.shape, F32)
    for at in chunks_of(slope_ref.shape[1]):
        dpre = (total(slots, at) * slope_ref[:, at]).astype(BF16)
        side += lax.dot_general(dpre, sb[:, at], ACROSS_DIMS, preferred_element_type=F32)
    up_ref[...] = side


def sides_kernel(n, *refs):
    up, down = refs[: n + 2], refs[n + 2 : 2 * n + 4]
    sb, sc, up_ref, down_ref, up_slots, down_slots, up_sems, down_sems = refs[2 * n + 4 :]
    copies = gathered_terms(up, up_slots, up_sems) + gathered_terms(down, down_slots, down_sems)
    for copy in copies:
        copy.wait()
    side_up = jnp.zeros(up_ref.shape, F32)
    side_down = jnp.zeros(down_ref.shape, F32)
    for at in chunks_of(up_slots.shape[2]):
        act, slope = gelu_terms(total(up_slots, at))
        dpre = (total(down_slots, at) * slope).astype(BF16)
        side_up += lax.dot_general(dpre, sb[:, at], ACROSS_DIMS, preferred_element_type=F32)
        side_down += lax.dot_general(act.astype(BF16), sc[:, at], ACROSS_DIMS, preferred_element_type=F32)
    up_ref[...] = side_up
    down_ref[...] = side_down


def side_call(kernel, jobs, others, outs, cost):
    quarter, units = jobs[0][0].shape
    n = len(jobs[0]) - 2
    vmem = pl.BlockSpec(memory_space=pltpu.VMEM)
    return pl.pallas_call(
        functools.partial(kernel, n),
        in_specs=[pl.BlockSpec(memory_space=pl.ANY)] * (len(jobs) * (n + 2)) + [vmem] * len(others),
        out_specs=[vmem] * len(outs),
        out_shape=outs,
        scratch_shapes=[pltpu.VMEM((3, quarter, units), BF16)] * len(jobs)
        + [pltpu.SemaphoreType.DMA((n + 2,))] * len(jobs),
        compiler_params=pltpu.CompilerParams(vmem_limit_bytes=24 * 2**20),
        cost_estimate=pl.CostEstimate(flops=int(cost), bytes_accessed=1000, transcendentals=0),
    )(*in_hbm(*[t for job in jobs for t in job]), *others)


SIBLING = [(0, 1), (1, 0), (2, 3), (3, 2)]
ACROSS = [(0, 2), (2, 0), (1, 3), (3, 1)]


def pipelined(normed, cotangent, w_up, w_down, sign_in_up, sign_out_up, sign_in_down, sign_out_down, patch_order):
    k = sign_in_up.shape[1]
    col = lax.axis_index("col")
    row = lax.axis_index("row")
    shard = normed.shape[0]
    quarter = shard // 4
    order = jnp.stack([3 - col, col ^ 1, col ^ 2, col]).astype(jnp.int32)
    inner = (row == 1) | (row == 2)

    def hop(a, pairs):
        return lax.ppermute(a, "row", pairs)

    def tie(a, *others):
        return lax.optimization_barrier((a, *others))[0]

    zero = jnp.zeros((1,), jnp.int32)
    pick = jnp.where(inner, 0, 1).astype(jnp.int32).reshape(1)
    PAIRS, MIDDLE, OUTER = [(0, 1), (1, 0), (2, 3), (3, 2)], [(1, 2), (2, 1)], [(1, 0), (2, 3)]
    sources = [row, row ^ 1, jnp.where(row < 2, 2, 1), jnp.where(row < 2, 3, 0)]
    weights = (w_up, w_down)
    bits = (sign_in_up.T, sign_out_down.T)
    shards = [normed, cotangent]
    products, received, outs, far, done = [], [], [], [], []

    def product(i, p, x, g, *after):
        if after:
            p = tie(p, *after)
        extra = (g, bits) if i % 2 == 0 else ()
        products.append(partial_product(p, order, g if i % 2 else x, weights[i % 2], i % 2, *extra))
        received.append([lax.ppermute(send, "col", SIBLING) for send in products[i][:PIECES]])

    def combine(i, after=None):
        got = received[i]
        if after is not None:
            got = tie(got, after)
        half = PIECES // 2
        outs.append((add_rows(products[i][PIECES], got[:half]), got[half:]))
        far.append(lax.ppermute(outs[i][0], "col", ACROSS))

    def terms(i):
        return (products[i][PIECES + 1], far[i], *outs[i][1])

    side = jax.ShapeDtypeStruct((quarter, k), F32)

    def finish(s):
        done.append(side_call(sides_kernel, [terms(2 * s), terms(2 * s + 1)], (sb, sc), [side] * 2, 1000))

    x, g = shards
    x1, x2 = hop(x, PAIRS), hop(x, MIDDLE)
    product(0, zero, (x, x), (g, g))
    combine(0)
    product(1, zero, (x, x), (g, g), outs[0][0], x1, x2)
    g1, g2 = hop(g, PAIRS), hop(g, MIDDLE)
    combine(1)
    product(2, zero, (x1, x1), (g1, g1), outs[1][0], far[0], g1, g2)
    x2b, x3 = hop(x2, OUTER), hop(tie(x1, products[1][0]), MIDDLE)
    sb, sc = both_signs(outs[1][0], sign_out_up.T, sign_in_down.T)
    combine(2)
    product(3, zero, (x1, x1), (g1, g1), outs[2][0], far[1], x2b, x3, sb, sc)
    g2b, g3 = hop(g2, OUTER), hop(tie(g1, products[2][0]), MIDDLE)
    finish(0)
    combine(3)
    product(4, pick, (x2, x2b), (g2, g2b), outs[3][0], far[2], done[0][0], g2b, g3)
    x3b = hop(tie(x3, products[3][0]), OUTER)
    combine(4)
    product(5, pick, (x2, x2b), (g2, g2b), outs[4][0], far[3], x3b)
    g3b = hop(tie(g3, products[4][0]), OUTER)
    finish(1)
    combine(5)
    product(6, pick, (x3, x3b), (g3, g3b), outs[5][0], far[4], done[1][0], g3b)
    combine(6)
    finish(2)
    product(7, pick, (x3, x3b), (g3, g3b), outs[6][0], far[5], done[2][0])
    combine(7)
    down, slope = side_call(
        act_kernel, [terms(6)], (sc,), [side, jax.ShapeDtypeStruct(outs[6][0].shape, F32)], ECOST
    )
    up = side_call(back_kernel, [terms(7)], (slope, sb), [side], 1000)[0]
    done.append((up, down))

    near = [products[2 * s][-1] for s in range(4)]
    near = tie(near, outs[7][0])
    got = lax.ppermute(jnp.stack([p[: 2 * quarter] for p in near]), "col", SIBLING)
    near = jnp.stack([p[2 * quarter :] for p in near]).astype(F32) + got.astype(F32)
    got = lax.ppermute(near[:, :quarter].astype(BF16), "col", ACROSS)
    proj = (near[:, quarter:] + got.astype(F32)).reshape(4 * quarter, 2 * k)

    table = members(patch_order)
    tables = [
        lax.dynamic_slice_in_dim(table, sources[s] * shard + col * quarter, quarter, 1) for s in range(4)
    ]
    side_up = jnp.concatenate([up for up, _ in done])
    side_down = jnp.concatenate([down for _, down in done])
    table = jnp.concatenate(tables, axis=1)
    high = lax.Precision.HIGHEST
    up = jnp.einsum("it,tk,tl->ikl", table, proj[:, :k], side_up, precision=high)
    down = jnp.einsum("it,tk,tl->ikl", table, side_down, proj[:, k:], precision=high)
    both = jnp.stack([up.reshape(IMAGES, 4, 4, -1), down.reshape(IMAGES, 4, 4, -1)]) * SCALE
    both = both.transpose(2, 3, 0, 1, 4)

    both = both.reshape(4, 2, 2, *both.shape[2:])
    chip, core = col // 2, col % 2
    mine = lax.dynamic_index_in_dim(both, chip, 1, keepdims=False)
    theirs = lax.dynamic_index_in_dim(both, 1 - chip, 1, keepdims=False)
    both = mine + lax.ppermute(theirs, "col", ACROSS)
    mine = lax.dynamic_index_in_dim(both, core, 1, keepdims=False)
    theirs = lax.dynamic_index_in_dim(both, 1 - core, 1, keepdims=False)
    both = mine + lax.ppermute(theirs, "col", SIBLING)
    total = lax.dynamic_index_in_dim(both, row, 0, keepdims=False)
    for off in (1, 2, 3):
        block = lax.dynamic_index_in_dim(both, row ^ off, 0, keepdims=False)
        total = total + hop(block, [(i, i ^ off) for i in range(4)])
    return total[0], total[1]


def solution(mesh):
    line = mesh.shape["row"] == 4 and mesh.shape["col"] == 4
    in_specs = (
        P(("parts", "row"), "col"),
        P(("parts", "row"), "col"),
        P("col", "row"),
        P("row", "col"),
        P("col", None),
        P("row", None),
        P("row", None),
        P("col", None),
        P("parts"),
    )
    out_specs = (P("parts", ("row", "col")), P("parts", ("row", "col")))
    return jax.shard_map(
        pipelined if line else gathered, mesh=mesh, in_specs=in_specs, out_specs=out_specs, check_vma=False
    )
```

```python
import functools

import jax
import jax.numpy as jnp
from jax import lax
from jax.experimental import pallas as pl
from jax.experimental.pallas import tpu as pltpu
from jax.sharding import PartitionSpec as P

D = 6144
FF = 24576
PATCHES = 256
IMAGES = 4
SCALE = 1.0 / (float(D) * float(FF) * float(PATCHES)) ** 0.5
BF16 = jnp.bfloat16
F32 = jnp.float32


def gelu_terms(pre):
    cdf = 0.5 * (1.0 + lax.erf(pre * 0.7071067811865476))
    pdf = jnp.exp(-0.5 * pre * pre) * 0.3989422804014327
    return pre * cdf, cdf + pre * pdf


def sign_matrix(bits):
    return (2 * bits - 1).astype(BF16)


def members(patch_order):
    images = patch_order // PATCHES
    return (images[None, :] == jnp.arange(IMAGES, dtype=jnp.int32)[:, None]).astype(F32)


def gathered(normed, cotangent, w_up, w_down, sign_in_up, sign_out_up, sign_in_down, sign_out_down, patch_order):
    k = sign_in_up.shape[1]
    x = lax.all_gather(normed, "row", axis=0, tiled=True)
    g = lax.all_gather(cotangent, "row", axis=0, tiled=True)
    up = jnp.dot(x, w_up, preferred_element_type=F32)
    down = lax.dot_general(g, w_down, (((1,), (1,)), ((), ())), preferred_element_type=F32)
    proj = jnp.concatenate(
        [
            jnp.dot(x, sign_matrix(sign_in_up), preferred_element_type=F32),
            jnp.dot(g, sign_matrix(sign_out_down), preferred_element_type=F32),
        ],
        axis=1,
    )
    pre = lax.psum_scatter(up.astype(BF16), "col", scatter_dimension=1, tiled=True).astype(F32)
    back = lax.psum_scatter(down.astype(BF16), "col", scatter_dimension=1, tiled=True).astype(F32)
    proj = lax.psum(proj.astype(BF16), "col").astype(F32)
    units = pre.shape[1]
    first = lax.axis_index("col") * units
    sb = sign_matrix(lax.dynamic_slice_in_dim(sign_out_up, first, units, 0))
    sc = sign_matrix(lax.dynamic_slice_in_dim(sign_in_down, first, units, 0))
    act, slope = gelu_terms(pre)
    side_up = jnp.dot((back * slope).astype(BF16), sb, preferred_element_type=F32)
    side_down = jnp.dot(act.astype(BF16), sc, preferred_element_type=F32)
    table = members(patch_order)
    high = lax.Precision.HIGHEST
    up = jnp.einsum("it,tk,tl->ikl", table, proj[:, :k], side_up, precision=high)
    down = jnp.einsum("it,tk,tl->ikl", table, side_down, proj[:, k:], precision=high)
    return tuple(
        lax.psum_scatter(t.reshape(IMAGES, -1) * SCALE, ("row", "col"), scatter_dimension=1, tiled=True)
        for t in (up, down)
    )


def columns(w_ref, contract, first, size):
    return w_ref.at[:, pl.ds(first, size)] if contract == 0 else w_ref.at[pl.ds(first, size), :]


def tiles_of(units):
    cuts, at = [], 0
    for _ in range(6):
        size = units // 6
        cuts.append((at, size))
        at += size
    return cuts if units % 1536 == 0 else [(0, units)]


def partial_kernel(contract, tiles, pick_ref, order_ref, *refs):
    n = 6 if contract == 0 else 2
    ins, w_ref, refs = refs[:n], refs[n], refs[n + 1 :]
    send_refs, (fwd_ref, keep_ref), refs = refs[:PIECES], refs[PIECES : PIECES + 2], refs[PIECES + 2 :]
    if contract == 0:
        rows, y_ref, w_v, row_sem, w_sem, out_sem, other, bits, other_sem, bits_sem = refs
    else:
        rows, y_ref, w_v, row_sem, w_sem, out_sem = refs
    quarter = rows.shape[0] // 4
    piece = 2 * quarter // PIECES
    parts = [(n * piece, piece, ref) for n, ref in enumerate(send_refs)]
    parts += [(2 * quarter, quarter, fwd_ref), (3 * quarter, quarter, keep_ref)]

    def row_copies(source, target, sem):
        return [
            pltpu.make_async_copy(
                source.at[pl.ds(pl.multiple_of(order_ref[j] * quarter, quarter), quarter), :],
                target.at[pl.ds(j * quarter, quarter), :],
                sem.at[j],
            )
            for j in range(4)
        ]

    for choice in (0, 1):

        @pl.when(pick_ref[0] == choice)
        def _():
            for copy in row_copies(ins[choice], rows, row_sem):
                copy.start()

    loads = [
        pltpu.make_async_copy(columns(w_ref, contract, *t), columns(w_v, contract, *t), w_sem.at[j])
        for j, t in enumerate(tiles)
    ]
    for copy in loads[:AHEAD]:
        copy.start()
    for copy in row_copies(ins[0], rows, row_sem):
        copy.wait()
    if contract == 0:
        for choice in (0, 1):

            @pl.when(pick_ref[0] == choice)
            def _():
                for copy in row_copies(ins[2 + choice], other, other_sem):
                    copy.start()

        bit_copies = [pltpu.make_async_copy(ins[4 + n], bits.at[n], bits_sem.at[n]) for n in range(2)]
        for copy in bit_copies:
            copy.start()
    outs = []

    def put(j, at):
        for n, (first, count, out) in enumerate(parts):
            copy = pltpu.make_async_copy(y_ref.at[pl.ds(first, count), at], out.at[:, at], out_sem.at[n, j])
            copy.start()
            outs.append(copy)

    for j, (first_unit, size) in enumerate(tiles):
        loads[j].wait()
        if j + AHEAD < len(tiles):
            loads[j + AHEAD].start()
        at = pl.ds(first_unit, size)
        y_ref[:, at] = lax.dot_general(
            rows[...],
            columns(w_v, contract, first_unit, size)[...],
            (((1,), (contract,)), ((), ())),
            preferred_element_type=F32,
        ).astype(BF16)
        put(j, at)
    if contract == 0:
        for copy in row_copies(ins[2], other, other_sem) + bit_copies:
            copy.wait()
        first_unit, size = tiles[-1]
        at = pl.ds(first_unit + size, 2 * bits.shape[1])
        y_ref[:, at] = jnp.concatenate(
            [
                lax.dot_general(
                    left[...], (2 * bits[n] - 1).astype(F32).astype(BF16), ACROSS_DIMS, preferred_element_type=F32
                )
                for n, left in enumerate((rows, other))
            ],
            axis=1,
        ).astype(BF16)
        put(len(tiles), at)
    for copy in outs:
        copy.wait()


ACROSS_DIMS = (((1,), (1,)), ((), ()))
COST = 4.8e9
ECOST = 2.6e9
AHEAD = 3
PIECES = 4


def in_hbm(*arrays):
    return [pltpu.with_memory_space_constraint(a, pltpu.HBM) for a in arrays]


def partial_product(pick, order, x, w, contract, g=None, bits=None):
    tokens, depth = x[0].shape
    units = w.shape[1 - contract]
    tiles = tiles_of(units)
    quarter = tokens // 4
    anywhere = pl.BlockSpec(memory_space=pl.ANY)
    scalars = pl.BlockSpec(memory_space=pltpu.SMEM)
    ins, scratch, width = [*x], [], units
    if g is not None:
        ins += [*g, *bits]
        width += 2 * bits[0].shape[0]
        scratch = [
            pltpu.VMEM((tokens, depth), BF16),
            pltpu.VMEM((2, *bits[0].shape), bits[0].dtype),
            pltpu.SemaphoreType.DMA((4,)),
            pltpu.SemaphoreType.DMA((2,)),
        ]
    ins = in_hbm(*ins, w)
    return pl.pallas_call(
        functools.partial(partial_kernel, contract, tiles),
        in_specs=[scalars, scalars] + [anywhere] * len(ins),
        out_specs=[anywhere] * (PIECES + 2),
        out_shape=[pltpu.HBM((2 * quarter // PIECES, width), BF16)] * PIECES
        + [pltpu.HBM((quarter, width), BF16)] * 2,
        scratch_shapes=[
            pltpu.VMEM((tokens, depth), BF16),
            pltpu.VMEM((tokens, width), BF16),
            pltpu.VMEM(w.shape, BF16),
            pltpu.SemaphoreType.DMA((4,)),
            pltpu.SemaphoreType.DMA((len(tiles),)),
            pltpu.SemaphoreType.DMA((PIECES + 2, len(tiles) + 1)),
        ]
        + scratch,
        compiler_params=pltpu.CompilerParams(vmem_limit_bytes=36 * 2**20),
        cost_estimate=pl.CostEstimate(flops=int(COST), bytes_accessed=1000, transcendentals=0),
    )(pick, order, *ins)


def add_kernel(a_ref, *refs):
    terms, (out_ref, slots, sems) = refs[:-3], refs[-3:]
    piece = terms[0].shape[0]
    copies = [pltpu.make_async_copy(a_ref, slots.at[0], sems.at[0])]
    for n, ref in enumerate(terms):
        copies.append(pltpu.make_async_copy(ref, slots.at[1, pl.ds(n * piece, piece), :], sems.at[1 + n]))
    for copy in copies:
        copy.start()
    for copy in copies:
        copy.wait()
    out_ref[...] = (slots[0].astype(F32) + slots[1].astype(F32)).astype(BF16)


def add_rows(a, b):
    return pl.pallas_call(
        add_kernel,
        in_specs=[pl.BlockSpec(memory_space=pl.ANY)] * (1 + len(b)),
        out_specs=pl.BlockSpec(memory_space=pltpu.VMEM),
        out_shape=jax.ShapeDtypeStruct(a.shape, BF16),
        scratch_shapes=[pltpu.VMEM((2, *a.shape), BF16), pltpu.SemaphoreType.DMA((1 + len(b),))],
        compiler_params=pltpu.CompilerParams(vmem_limit_bytes=16 * 2**20),
        cost_estimate=pl.CostEstimate(flops=1000, bytes_accessed=1000, transcendentals=0),
    )(a, *b)


def gathered_terms(refs, slots, sems):
    piece = refs[2].shape[0]
    copies = [
        pltpu.make_async_copy(refs[0], slots.at[0], sems.at[0]),
        pltpu.make_async_copy(refs[1], slots.at[1], sems.at[1]),
    ]
    for n, ref in enumerate(refs[2:]):
        copies.append(pltpu.make_async_copy(ref, slots.at[2, pl.ds(n * piece, piece), :], sems.at[2 + n]))
    for copy in copies:
        copy.start()
    return copies


def total(slots, at):
    return slots[0, :, at].astype(F32) + slots[1, :, at].astype(F32) + slots[2, :, at].astype(F32)


def chunks_of(units):
    chunk = 1024 if units % 1024 == 0 else units
    return [pl.ds(j * chunk, chunk) for j in range(units // chunk)]


def act_kernel(n, *refs):
    terms, (sc, down_ref, slope_ref, proj_ref, slots, sems) = refs[:n], refs[n:]
    for copy in gathered_terms(terms, slots, sems):
        copy.wait()
    side = jnp.zeros(down_ref.shape, F32)
    units = slope_ref.shape[1]
    for at in chunks_of(units):
        act, slope = gelu_terms(total(slots, at))
        side += lax.dot_general(act.astype(BF16), sc[:, at], ACROSS_DIMS, preferred_element_type=F32)
        slope_ref[:, at] = slope
    down_ref[...] = side
    proj_ref[...] = total(slots, pl.ds(units, proj_ref.shape[1]))


def back_kernel(n, *refs):
    terms, (slope_ref, sb, up_ref, slots, sems) = refs[:n], refs[n:]
    for copy in gathered_terms(terms, slots, sems):
        copy.wait()
    side = jnp.zeros(up_ref.shape, F32)
    for at in chunks_of(slope_ref.shape[1]):
        dpre = (total(slots, at) * slope_ref[:, at]).astype(BF16)
        side += lax.dot_general(dpre, sb[:, at], ACROSS_DIMS, preferred_element_type=F32)
    up_ref[...] = side


def sides_kernel(n, steps, *refs):
    terms = refs[: 2 * n * steps]
    b_ref, c_ref, up_ref, down_ref, proj_ref, sb, sc, ups, downs, bits, sems, bit_sems = refs[2 * n * steps :]
    quarter, units = downs.shape[2:]
    bit_copies = [
        pltpu.make_async_copy(b_ref, bits.at[0], bit_sems.at[0]),
        pltpu.make_async_copy(c_ref, bits.at[1], bit_sems.at[1]),
    ]
    for copy in bit_copies:
        copy.start()

    def fetch(s):
        up, down = terms[2 * n * s : 2 * n * s + n], terms[2 * n * s + n : 2 * n * s + 2 * n]
        return gathered_terms(up, ups.at[s % 2], sems.at[s, 0]) + gathered_terms(down, downs.at[s % 2], sems.at[s, 1])

    coming = fetch(0)
    for copy in bit_copies:
        copy.wait()
    sb[...] = (2 * bits[0] - 1).astype(F32).astype(BF16)
    sc[...] = (2 * bits[1] - 1).astype(F32).astype(BF16)
    for s in range(steps):
        for copy in coming:
            copy.wait()
        if s + 1 < steps:
            coming = fetch(s + 1)
        side_up = jnp.zeros((quarter, up_ref.shape[1]), F32)
        side_down = jnp.zeros((quarter, up_ref.shape[1]), F32)
        for at in chunks_of(units):
            act, slope = gelu_terms(total(ups.at[s % 2], at))
            dpre = (total(downs.at[s % 2], at) * slope).astype(BF16)
            side_up += lax.dot_general(dpre, sb[:, at], ACROSS_DIMS, preferred_element_type=F32)
            side_down += lax.dot_general(act.astype(BF16), sc[:, at], ACROSS_DIMS, preferred_element_type=F32)
        mine = slice(s * quarter, (s + 1) * quarter)
        up_ref[mine] = side_up
        down_ref[mine] = side_down
        proj_ref[mine] = total(ups.at[s % 2], pl.ds(units, proj_ref.shape[1]))


def side_call(kernel, terms, others, outs, scratch, cost):
    vmem, anywhere = pl.BlockSpec(memory_space=pltpu.VMEM), pl.BlockSpec(memory_space=pl.ANY)
    others, in_vmem = zip(*others)
    return pl.pallas_call(
        kernel,
        in_specs=[anywhere] * len(terms) + [vmem if v else anywhere for v in in_vmem],
        out_specs=[vmem] * len(outs),
        out_shape=outs,
        scratch_shapes=scratch,
        compiler_params=pltpu.CompilerParams(vmem_limit_bytes=24 * 2**20),
        cost_estimate=pl.CostEstimate(flops=int(cost), bytes_accessed=1000, transcendentals=0),
    )(*in_hbm(*terms), *others)


SIBLING = [(0, 1), (1, 0), (2, 3), (3, 2)]
ACROSS = [(0, 2), (2, 0), (1, 3), (3, 1)]


def pipelined(normed, cotangent, w_up, w_down, sign_in_up, sign_out_up, sign_in_down, sign_out_down, patch_order):
    k = sign_in_up.shape[1]
    col = lax.axis_index("col")
    row = lax.axis_index("row")
    shard = normed.shape[0]
    quarter = shard // 4
    order = jnp.stack([3 - col, col ^ 1, col ^ 2, col]).astype(jnp.int32)
    inner = (row == 1) | (row == 2)

    def hop(a, pairs):
        return lax.ppermute(a, "row", pairs)

    def tie(a, *others):
        return lax.optimization_barrier((a, *others))[0]

    zero = jnp.zeros((1,), jnp.int32)
    pick = jnp.where(inner, 0, 1).astype(jnp.int32).reshape(1)
    PAIRS, MIDDLE, OUTER = [(0, 1), (1, 0), (2, 3), (3, 2)], [(1, 2), (2, 1)], [(1, 0), (2, 3)]
    sources = [row, row ^ 1, jnp.where(row < 2, 2, 1), jnp.where(row < 2, 3, 0)]
    weights = (w_up, w_down)
    bits = (sign_in_up.T, sign_out_down.T)
    shards = [normed, cotangent]
    products, received, outs, far = [], [], [], []

    def product(i, p, x, g, *after):
        if after:
            p = tie(p, *after)
        extra = (g, bits) if i % 2 == 0 else ()
        products.append(partial_product(p, order, g if i % 2 else x, weights[i % 2], i % 2, *extra))
        received.append([lax.ppermute(send, "col", SIBLING) for send in products[i][:PIECES]])

    def combine(i, after=None):
        got = received[i]
        if after is not None:
            got = tie(got, after)
        half = PIECES // 2
        outs.append((add_rows(products[i][PIECES], got[:half]), got[half:]))
        far.append(lax.ppermute(outs[i][0], "col", ACROSS))

    def terms(i):
        return (products[i][PIECES + 1], far[i], *outs[i][1])

    x, g = shards
    x1, x2 = hop(x, PAIRS), hop(x, MIDDLE)
    product(0, zero, (x, x), (g, g))
    combine(0)
    product(1, zero, (x, x), (g, g), outs[0][0], x1, x2)
    g1, g2 = hop(g, PAIRS), hop(g, MIDDLE)
    combine(1)
    product(2, zero, (x1, x1), (g1, g1), outs[1][0], far[0], g1, g2)
    x2b, x3 = hop(x2, OUTER), hop(tie(x1, products[1][0]), MIDDLE)
    combine(2)
    product(3, zero, (x1, x1), (g1, g1), outs[2][0], far[1], x2b, x3)
    g2b, g3 = hop(g2, OUTER), hop(tie(g1, products[2][0]), MIDDLE)
    combine(3)
    product(4, pick, (x2, x2b), (g2, g2b), outs[3][0], far[2], g2b, g3)
    x3b = hop(tie(x3, products[3][0]), OUTER)
    combine(4)
    product(5, pick, (x2, x2b), (g2, g2b), outs[4][0], far[3], x3b)
    g3b = hop(tie(g3, products[4][0]), OUTER)
    combine(5)
    product(6, pick, (x3, x3b), (g3, g3b), outs[5][0], far[4], g3b)
    combine(6)
    product(7, pick, (x3, x3b), (g3, g3b), outs[6][0], far[5])
    combine(7, far[6])
    n, units = len(terms(0)), w_up.shape[1]
    b, c = tie((sign_out_up, sign_in_down), outs[7][0])
    early = 3 * quarter
    sides_up, sides_down, projs, sb, sc = side_call(
        functools.partial(sides_kernel, n, 3),
        [t for i in range(6) for t in terms(i)],
        [(b.T, False), (c.T, False)],
        [jax.ShapeDtypeStruct((early, k), F32)] * 2
        + [jax.ShapeDtypeStruct((early, 2 * k), F32)]
        + [jax.ShapeDtypeStruct((k, units), BF16)] * 2,
        [
            pltpu.VMEM((2, 3, quarter, units + 2 * k), BF16),
            pltpu.VMEM((2, 3, quarter, units), BF16),
            pltpu.VMEM((2, k, units), jnp.int32),
            pltpu.SemaphoreType.DMA((3, 2, n)),
            pltpu.SemaphoreType.DMA((2,)),
        ],
        1000,
    )
    down, slope, last = side_call(
        functools.partial(act_kernel, n),
        terms(6),
        [(sc, True)],
        [
            jax.ShapeDtypeStruct((quarter, k), F32),
            jax.ShapeDtypeStruct((quarter, units), F32),
            jax.ShapeDtypeStruct((quarter, 2 * k), F32),
        ],
        [pltpu.VMEM((3, quarter, units + 2 * k), BF16), pltpu.SemaphoreType.DMA((n,))],
        ECOST,
    )
    up = side_call(
        functools.partial(back_kernel, n),
        terms(7),
        [(slope, True), (sb, True)],
        [jax.ShapeDtypeStruct((quarter, k), F32)],
        [pltpu.VMEM((3, quarter, units), BF16), pltpu.SemaphoreType.DMA((n,))],
        1000,
    )[0]
    side_up = jnp.concatenate([sides_up, up])
    side_down = jnp.concatenate([sides_down, down])
    proj = jnp.concatenate([projs, last])

    table = members(patch_order)
    tables = [
        lax.dynamic_slice_in_dim(table, sources[s] * shard + col * quarter, quarter, 1) for s in range(4)
    ]
    table = jnp.concatenate(tables, axis=1)
    high = lax.Precision.HIGHEST
    up = jnp.einsum("it,tk,tl->ikl", table, proj[:, :k], side_up, precision=high)
    down = jnp.einsum("it,tk,tl->ikl", table, side_down, proj[:, k:], precision=high)
    both = jnp.stack([up.reshape(IMAGES, 4, 4, -1), down.reshape(IMAGES, 4, 4, -1)]) * SCALE
    both = both.transpose(2, 3, 0, 1, 4)

    both = both.reshape(4, 2, 2, *both.shape[2:])
    chip, core = col // 2, col % 2
    mine = lax.dynamic_index_in_dim(both, chip, 1, keepdims=False)
    theirs = lax.dynamic_index_in_dim(both, 1 - chip, 1, keepdims=False)
    both = mine + lax.ppermute(theirs, "col", ACROSS)
    mine = lax.dynamic_index_in_dim(both, core, 1, keepdims=False)
    theirs = lax.dynamic_index_in_dim(both, 1 - core, 1, keepdims=False)
    both = mine + lax.ppermute(theirs, "col", SIBLING)
    total = lax.dynamic_index_in_dim(both, row, 0, keepdims=False)
    for off in (1, 2, 3):
        block = lax.dynamic_index_in_dim(both, row ^ off, 0, keepdims=False)
        total = total + hop(block, [(i, i ^ off) for i in range(4)])
    return total[0], total[1]


def solution(mesh):
    line = mesh.shape["row"] == 4 and mesh.shape["col"] == 4
    in_specs = (
        P(("parts", "row"), "col"),
        P(("parts", "row"), "col"),
        P("col", "row"),
        P("row", "col"),
        P("col", None),
        P("row", None),
        P("row", None),
        P("col", None),
        P("parts"),
    )
    out_specs = (P("parts", ("row", "col")), P("parts", ("row", "col")))
    return jax.shard_map(
        pipelined if line else gathered, mesh=mesh, in_specs=in_specs, out_specs=out_specs, check_vma=False
    )
```

```python
import functools

import jax
import jax.numpy as jnp
from jax import lax
from jax.experimental import pallas as pl
from jax.experimental.pallas import tpu as pltpu
from jax.sharding import PartitionSpec as P

D = 6144
FF = 24576
PATCHES = 256
IMAGES = 4
SCALE = 1.0 / (float(D) * float(FF) * float(PATCHES)) ** 0.5
BF16 = jnp.bfloat16
F32 = jnp.float32


def gelu_terms(pre):
    cdf = 0.5 * (1.0 + lax.erf(pre * 0.7071067811865476))
    pdf = jnp.exp(-0.5 * pre * pre) * 0.3989422804014327
    return pre * cdf, cdf + pre * pdf


def sign_matrix(bits):
    return (2 * bits - 1).astype(BF16)


def members(patch_order):
    images = patch_order // PATCHES
    return (images[None, :] == jnp.arange(IMAGES, dtype=jnp.int32)[:, None]).astype(F32)


def gathered(normed, cotangent, w_up, w_down, sign_in_up, sign_out_up, sign_in_down, sign_out_down, patch_order):
    k = sign_in_up.shape[1]
    x = lax.all_gather(normed, "row", axis=0, tiled=True)
    g = lax.all_gather(cotangent, "row", axis=0, tiled=True)
    up = jnp.dot(x, w_up, preferred_element_type=F32)
    down = lax.dot_general(g, w_down, (((1,), (1,)), ((), ())), preferred_element_type=F32)
    proj = jnp.concatenate(
        [
            jnp.dot(x, sign_matrix(sign_in_up), preferred_element_type=F32),
            jnp.dot(g, sign_matrix(sign_out_down), preferred_element_type=F32),
        ],
        axis=1,
    )
    pre = lax.psum_scatter(up.astype(BF16), "col", scatter_dimension=1, tiled=True).astype(F32)
    back = lax.psum_scatter(down.astype(BF16), "col", scatter_dimension=1, tiled=True).astype(F32)
    proj = lax.psum(proj.astype(BF16), "col").astype(F32)
    units = pre.shape[1]
    first = lax.axis_index("col") * units
    sb = sign_matrix(lax.dynamic_slice_in_dim(sign_out_up, first, units, 0))
    sc = sign_matrix(lax.dynamic_slice_in_dim(sign_in_down, first, units, 0))
    act, slope = gelu_terms(pre)
    side_up = jnp.dot((back * slope).astype(BF16), sb, preferred_element_type=F32)
    side_down = jnp.dot(act.astype(BF16), sc, preferred_element_type=F32)
    table = members(patch_order)
    high = lax.Precision.HIGHEST
    up = jnp.einsum("it,tk,tl->ikl", table, proj[:, :k], side_up, precision=high)
    down = jnp.einsum("it,tk,tl->ikl", table, side_down, proj[:, k:], precision=high)
    return tuple(
        lax.psum_scatter(t.reshape(IMAGES, -1) * SCALE, ("row", "col"), scatter_dimension=1, tiled=True)
        for t in (up, down)
    )


def columns(w_ref, contract, j, tile):
    at = pl.ds(pl.multiple_of(j * tile, tile), tile)
    return w_ref.at[:, at] if contract == 0 else w_ref.at[at, :]


def partial_kernel(contract, tile, pick_ref, order_ref, *refs):
    n = 6 if contract == 0 else 2
    ins, w_ref, refs = refs[:n], refs[n], refs[n + 1 :]
    send_refs, (fwd_ref, keep_ref), refs = refs[:PIECES], refs[PIECES : PIECES + 2], refs[PIECES + 2 :]
    if contract == 0:
        rows, y_ref, w_v, row_sem, w_sem, out_sem, other, bits, other_sem, bits_sem = refs
    else:
        rows, y_ref, w_v, row_sem, w_sem, out_sem = refs
    tiles = w_ref.shape[1 - contract] // tile
    quarter = rows.shape[0] // 4
    piece = 2 * quarter // PIECES
    parts = [(n * piece, piece, ref) for n, ref in enumerate(send_refs)]
    parts += [(2 * quarter, quarter, fwd_ref), (3 * quarter, quarter, keep_ref)]

    def row_copies(source, target, sem):
        return [
            pltpu.make_async_copy(
                source.at[pl.ds(pl.multiple_of(order_ref[j] * quarter, quarter), quarter), :],
                target.at[pl.ds(j * quarter, quarter), :],
                sem.at[j],
            )
            for j in range(4)
        ]

    for choice in (0, 1):

        @pl.when(pick_ref[0] == choice)
        def _():
            for copy in row_copies(ins[choice], rows, row_sem):
                copy.start()

    def load(j):
        return pltpu.make_async_copy(columns(w_ref, contract, j, tile), columns(w_v, contract, j, tile), w_sem.at[j])

    def puts(j, at):
        return [
            pltpu.make_async_copy(y_ref.at[pl.ds(first, count), at], out.at[:, at], out_sem.at[n, j])
            for n, (first, count, out) in enumerate(parts)
        ]

    def span(j):
        return pl.ds(pl.multiple_of(j * tile, tile), tile)

    for j in range(min(AHEAD, tiles)):
        load(j).start()
    for copy in row_copies(ins[0], rows, row_sem):
        copy.wait()
    if contract == 0:
        for choice in (0, 1):

            @pl.when(pick_ref[0] == choice)
            def _():
                for copy in row_copies(ins[2 + choice], other, other_sem):
                    copy.start()

        bit_copies = [pltpu.make_async_copy(ins[4 + n], bits.at[n], bits_sem.at[n]) for n in range(2)]
        for copy in bit_copies:
            copy.start()

    @pl.loop(0, tiles)
    def _(j):
        load(j).wait()

        @pl.when(j + AHEAD < tiles)
        def _():
            load(j + AHEAD).start()

        y_ref[:, span(j)] = lax.dot_general(
            rows[...],
            columns(w_v, contract, j, tile)[...],
            (((1,), (contract,)), ((), ())),
            preferred_element_type=F32,
        ).astype(BF16)
        for copy in puts(j, span(j)):
            copy.start()

    last = []
    if contract == 0:
        for copy in row_copies(ins[2], other, other_sem) + bit_copies:
            copy.wait()
        at = pl.ds(tiles * tile, 2 * bits.shape[1])
        y_ref[:, at] = jnp.concatenate(
            [
                lax.dot_general(
                    left[...], (2 * bits[n] - 1).astype(F32).astype(BF16), ACROSS_DIMS, preferred_element_type=F32
                )
                for n, left in enumerate((rows, other))
            ],
            axis=1,
        ).astype(BF16)
        last = puts(tiles, at)
        for copy in last:
            copy.start()

    @pl.loop(0, tiles)
    def _(j):
        for copy in puts(j, span(j)):
            copy.wait()

    for copy in last:
        copy.wait()


ACROSS_DIMS = (((1,), (1,)), ((), ()))
COST = 4.8e9
ECOST = 2.6e9
AHEAD = 3
PIECES = 4


def in_hbm(*arrays):
    return [pltpu.with_memory_space_constraint(a, pltpu.HBM) for a in arrays]


def partial_product(pick, order, x, w, contract, g=None, bits=None):
    tokens, depth = x[0].shape
    units = w.shape[1 - contract]
    tile = 1024 if units % 1024 == 0 else units
    tiles = units // tile
    quarter = tokens // 4
    anywhere = pl.BlockSpec(memory_space=pl.ANY)
    scalars = pl.BlockSpec(memory_space=pltpu.SMEM)
    ins, scratch, width = [*x], [], units
    if g is not None:
        ins += [*g, *bits]
        width += 2 * bits[0].shape[0]
        scratch = [
            pltpu.VMEM((tokens, depth), BF16),
            pltpu.VMEM((2, *bits[0].shape), bits[0].dtype),
            pltpu.SemaphoreType.DMA((4,)),
            pltpu.SemaphoreType.DMA((2,)),
        ]
    ins = in_hbm(*ins, w)
    return pl.pallas_call(
        functools.partial(partial_kernel, contract, tile),
        in_specs=[scalars, scalars] + [anywhere] * len(ins),
        out_specs=[anywhere] * (PIECES + 2),
        out_shape=[pltpu.HBM((2 * quarter // PIECES, width), BF16)] * PIECES
        + [pltpu.VMEM((quarter, width), BF16), pltpu.HBM((quarter, width), BF16)],
        scratch_shapes=[
            pltpu.VMEM((tokens, depth), BF16),
            pltpu.VMEM((tokens, width), BF16),
            pltpu.VMEM(w.shape, BF16),
            pltpu.SemaphoreType.DMA((4,)),
            pltpu.SemaphoreType.DMA((tiles,)),
            pltpu.SemaphoreType.DMA((PIECES + 2, tiles + 1)),
        ]
        + scratch,
        compiler_params=pltpu.CompilerParams(vmem_limit_bytes=36 * 2**20),
        cost_estimate=pl.CostEstimate(flops=int(COST), bytes_accessed=1000, transcendentals=0),
    )(pick, order, *ins)


def add_kernel(a_ref, *refs):
    terms, (out_ref, slots, sems) = refs[:-3], refs[-3:]
    piece = terms[0].shape[0]
    copies = [pltpu.make_async_copy(a_ref, slots.at[0], sems.at[0])]
    for n, ref in enumerate(terms):
        copies.append(pltpu.make_async_copy(ref, slots.at[1, pl.ds(n * piece, piece), :], sems.at[1 + n]))
    for copy in copies:
        copy.start()
    for copy in copies:
        copy.wait()
    out_ref[...] = (slots[0].astype(F32) + slots[1].astype(F32)).astype(BF16)


def add_rows(a, b):
    return pl.pallas_call(
        add_kernel,
        in_specs=[pl.BlockSpec(memory_space=pl.ANY)] * (1 + len(b)),
        out_specs=pl.BlockSpec(memory_space=pltpu.VMEM),
        out_shape=jax.ShapeDtypeStruct(a.shape, BF16),
        scratch_shapes=[pltpu.VMEM((2, *a.shape), BF16), pltpu.SemaphoreType.DMA((1 + len(b),))],
        compiler_params=pltpu.CompilerParams(vmem_limit_bytes=16 * 2**20),
        cost_estimate=pl.CostEstimate(flops=1000, bytes_accessed=1000, transcendentals=0),
    )(pltpu.with_memory_space_constraint(a, pltpu.VMEM), *b)


def gathered_terms(refs, slots, sems):
    piece = refs[2].shape[0]
    copies = [
        pltpu.make_async_copy(refs[0], slots.at[0], sems.at[0]),
        pltpu.make_async_copy(refs[1], slots.at[1], sems.at[1]),
    ]
    for n, ref in enumerate(refs[2:]):
        copies.append(pltpu.make_async_copy(ref, slots.at[2, pl.ds(n * piece, piece), :], sems.at[2 + n]))
    for copy in copies:
        copy.start()
    return copies


def total(slots, at):
    return slots[0, :, at].astype(F32) + slots[1, :, at].astype(F32) + slots[2, :, at].astype(F32)


def over_chunks(units, body, init):
    chunk = 1024 if units % 1024 == 0 else units
    return lax.fori_loop(0, units // chunk, lambda j, c: body(pl.ds(pl.multiple_of(j * chunk, chunk), chunk), c), init)


def act_kernel(n, *refs):
    terms, (sc, down_ref, slope_ref, proj_ref, slots, sems) = refs[:n], refs[n:]
    for copy in gathered_terms(terms, slots, sems):
        copy.wait()
    units = slope_ref.shape[1]

    def body(at, side):
        act, slope = gelu_terms(total(slots, at))
        slope_ref[:, at] = slope
        return side + lax.dot_general(act.astype(BF16), sc[:, at], ACROSS_DIMS, preferred_element_type=F32)

    down_ref[...] = over_chunks(units, body, jnp.zeros(down_ref.shape, F32))
    proj_ref[...] = total(slots, pl.ds(units, proj_ref.shape[1]))


def back_kernel(n, *refs):
    terms, (slope_ref, sb, up_ref, slots, sems) = refs[:n], refs[n:]
    for copy in gathered_terms(terms, slots, sems):
        copy.wait()

    def body(at, side):
        dpre = (total(slots, at) * slope_ref[:, at]).astype(BF16)
        return side + lax.dot_general(dpre, sb[:, at], ACROSS_DIMS, preferred_element_type=F32)

    up_ref[...] = over_chunks(slope_ref.shape[1], body, jnp.zeros(up_ref.shape, F32))


def sides_kernel(n, steps, *refs):
    terms = refs[: 2 * n * steps]
    b_ref, c_ref, up_ref, down_ref, proj_ref, sb, sc, ups, downs, bits, sems, bit_sems = refs[2 * n * steps :]
    quarter, units = downs.shape[2:]
    bit_copies = [
        pltpu.make_async_copy(b_ref, bits.at[0], bit_sems.at[0]),
        pltpu.make_async_copy(c_ref, bits.at[1], bit_sems.at[1]),
    ]
    for copy in bit_copies:
        copy.start()

    def fetch(s):
        up, down = terms[2 * n * s : 2 * n * s + n], terms[2 * n * s + n : 2 * n * s + 2 * n]
        return gathered_terms(up, ups.at[s % 2], sems.at[s, 0]) + gathered_terms(down, downs.at[s % 2], sems.at[s, 1])

    coming = fetch(0)
    for copy in bit_copies:
        copy.wait()
    sb[...] = (2 * bits[0] - 1).astype(F32).astype(BF16)
    sc[...] = (2 * bits[1] - 1).astype(F32).astype(BF16)
    for s in range(steps):
        for copy in coming:
            copy.wait()
        if s + 1 < steps:
            coming = fetch(s + 1)

        def body(at, both):
            act, slope = gelu_terms(total(ups.at[s % 2], at))
            dpre = (total(downs.at[s % 2], at) * slope).astype(BF16)
            return (
                both[0] + lax.dot_general(dpre, sb[:, at], ACROSS_DIMS, preferred_element_type=F32),
                both[1] + lax.dot_general(act.astype(BF16), sc[:, at], ACROSS_DIMS, preferred_element_type=F32),
            )

        zeros = jnp.zeros((quarter, up_ref.shape[1]), F32)
        side_up, side_down = over_chunks(units, body, (zeros, zeros))
        mine = slice(s * quarter, (s + 1) * quarter)
        up_ref[mine] = side_up
        down_ref[mine] = side_down
        proj_ref[mine] = total(ups.at[s % 2], pl.ds(units, proj_ref.shape[1]))


def side_call(kernel, terms, others, outs, scratch, cost):
    vmem, anywhere = pl.BlockSpec(memory_space=pltpu.VMEM), pl.BlockSpec(memory_space=pl.ANY)
    others, in_vmem = zip(*others)
    return pl.pallas_call(
        kernel,
        in_specs=[anywhere] * len(terms) + [vmem if v else anywhere for v in in_vmem],
        out_specs=[vmem] * len(outs),
        out_shape=outs,
        scratch_shapes=scratch,
        compiler_params=pltpu.CompilerParams(vmem_limit_bytes=24 * 2**20),
        cost_estimate=pl.CostEstimate(flops=int(cost), bytes_accessed=1000, transcendentals=0),
    )(*in_hbm(*terms), *others)


SIBLING = [(0, 1), (1, 0), (2, 3), (3, 2)]
ACROSS = [(0, 2), (2, 0), (1, 3), (3, 1)]


def pipelined(normed, cotangent, w_up, w_down, sign_in_up, sign_out_up, sign_in_down, sign_out_down, patch_order):
    k = sign_in_up.shape[1]
    col = lax.axis_index("col")
    row = lax.axis_index("row")
    shard = normed.shape[0]
    quarter = shard // 4
    order = jnp.stack([3 - col, col ^ 1, col ^ 2, col]).astype(jnp.int32)
    inner = (row == 1) | (row == 2)

    def hop(a, pairs):
        return lax.ppermute(a, "row", pairs)

    def tie(a, *others):
        return lax.optimization_barrier((a, *others))[0]

    zero = jnp.zeros((1,), jnp.int32)
    pick = jnp.where(inner, 0, 1).astype(jnp.int32).reshape(1)
    PAIRS, MIDDLE, OUTER = [(0, 1), (1, 0), (2, 3), (3, 2)], [(1, 2), (2, 1)], [(1, 0), (2, 3)]
    sources = [row, row ^ 1, jnp.where(row < 2, 2, 1), jnp.where(row < 2, 3, 0)]
    weights = (w_up, w_down)
    bits = (sign_in_up.T, sign_out_down.T)
    shards = [normed, cotangent]
    products, received, outs, far = [], [], [], []

    def product(i, p, x, g, *after):
        if after:
            p = tie(p, *after)
        extra = (g, bits) if i % 2 == 0 else ()
        products.append(partial_product(p, order, g if i % 2 else x, weights[i % 2], i % 2, *extra))
        received.append([lax.ppermute(send, "col", SIBLING) for send in products[i][:PIECES]])

    def combine(i, after=None):
        got = received[i]
        if after is not None:
            got = tie(got, after)
        half = PIECES // 2
        outs.append((add_rows(products[i][PIECES], got[:half]), got[half:]))
        far.append(lax.ppermute(outs[i][0], "col", ACROSS))

    def terms(i):
        return (products[i][PIECES + 1], far[i], *outs[i][1])

    x, g = shards
    x1, x2 = hop(x, PAIRS), hop(x, MIDDLE)
    product(0, zero, (x, x), (g, g))
    combine(0)
    product(1, zero, (x, x), (g, g), outs[0][0], x1, x2)
    g1, g2 = hop(g, PAIRS), hop(g, MIDDLE)
    combine(1)
    product(2, zero, (x1, x1), (g1, g1), outs[1][0], far[0], g1, g2)
    x2b, x3 = hop(x2, OUTER), hop(tie(x1, products[1][0]), MIDDLE)
    combine(2)
    product(3, zero, (x1, x1), (g1, g1), outs[2][0], far[1], x2b, x3)
    g2b, g3 = hop(g2, OUTER), hop(tie(g1, products[2][0]), MIDDLE)
    combine(3)
    product(4, pick, (x2, x2b), (g2, g2b), outs[3][0], far[2], g2b, g3)
    x3b = hop(tie(x3, products[3][0]), OUTER)
    combine(4)
    product(5, pick, (x2, x2b), (g2, g2b), outs[4][0], far[3], x3b)
    g3b = hop(tie(g3, products[4][0]), OUTER)
    combine(5)
    product(6, pick, (x3, x3b), (g3, g3b), outs[5][0], far[4], g3b)
    combine(6)
    product(7, pick, (x3, x3b), (g3, g3b), outs[6][0], far[5])
    combine(7, far[6])
    n, units = len(terms(0)), w_up.shape[1]
    b, c = tie((sign_out_up, sign_in_down), outs[7][0])
    early = 3 * quarter
    sides_up, sides_down, projs, sb, sc = side_call(
        functools.partial(sides_kernel, n, 3),
        [t for i in range(6) for t in terms(i)],
        [(b.T, False), (c.T, False)],
        [jax.ShapeDtypeStruct((early, k), F32)] * 2
        + [jax.ShapeDtypeStruct((early, 2 * k), F32)]
        + [jax.ShapeDtypeStruct((k, units), BF16)] * 2,
        [
            pltpu.VMEM((2, 3, quarter, units + 2 * k), BF16),
            pltpu.VMEM((2, 3, quarter, units), BF16),
            pltpu.VMEM((2, k, units), jnp.int32),
            pltpu.SemaphoreType.DMA((3, 2, n)),
            pltpu.SemaphoreType.DMA((2,)),
        ],
        1000,
    )
    down, slope, last = side_call(
        functools.partial(act_kernel, n),
        terms(6),
        [(sc, True)],
        [
            jax.ShapeDtypeStruct((quarter, k), F32),
            jax.ShapeDtypeStruct((quarter, units), F32),
            jax.ShapeDtypeStruct((quarter, 2 * k), F32),
        ],
        [pltpu.VMEM((3, quarter, units + 2 * k), BF16), pltpu.SemaphoreType.DMA((n,))],
        ECOST,
    )
    up = side_call(
        functools.partial(back_kernel, n),
        terms(7),
        [(slope, True), (sb, True)],
        [jax.ShapeDtypeStruct((quarter, k), F32)],
        [pltpu.VMEM((3, quarter, units), BF16), pltpu.SemaphoreType.DMA((n,))],
        1000,
    )[0]
    side_up = jnp.concatenate([sides_up, up])
    side_down = jnp.concatenate([sides_down, down])
    proj = jnp.concatenate([projs, last])

    table = members(patch_order)
    tables = [
        lax.dynamic_slice_in_dim(table, sources[s] * shard + col * quarter, quarter, 1) for s in range(4)
    ]
    table = jnp.concatenate(tables, axis=1)
    high = lax.Precision.HIGHEST
    up = jnp.einsum("it,tk,tl->ikl", table, proj[:, :k], side_up, precision=high)
    down = jnp.einsum("it,tk,tl->ikl", table, side_down, proj[:, k:], precision=high)
    both = jnp.stack([up.reshape(IMAGES, 4, 4, -1), down.reshape(IMAGES, 4, 4, -1)]) * SCALE
    both = both.transpose(2, 3, 0, 1, 4)

    both = both.reshape(4, 2, 2, *both.shape[2:])
    chip, core = col // 2, col % 2
    mine = lax.dynamic_index_in_dim(both, chip, 1, keepdims=False)
    theirs = lax.dynamic_index_in_dim(both, 1 - chip, 1, keepdims=False)
    both = mine + lax.ppermute(theirs, "col", ACROSS)
    mine = lax.dynamic_index_in_dim(both, core, 1, keepdims=False)
    theirs = lax.dynamic_index_in_dim(both, 1 - core, 1, keepdims=False)
    both = mine + lax.ppermute(theirs, "col", SIBLING)
    total = lax.dynamic_index_in_dim(both, row, 0, keepdims=False)
    for off in (1, 2, 3):
        block = lax.dynamic_index_in_dim(both, row ^ off, 0, keepdims=False)
        total = total + hop(block, [(i, i ^ off) for i in range(4)])
    return total[0], total[1]


def solution(mesh):
    line = mesh.shape["row"] == 4 and mesh.shape["col"] == 4
    in_specs = (
        P(("parts", "row"), "col"),
        P(("parts", "row"), "col"),
        P("col", "row"),
        P("row", "col"),
        P("col", None),
        P("row", None),
        P("row", None),
        P("col", None),
        P("parts"),
    )
    out_specs = (P("parts", ("row", "col")), P("parts", ("row", "col")))
    return jax.shard_map(
        pipelined if line else gathered, mesh=mesh, in_specs=in_specs, out_specs=out_specs, check_vma=False
    )
```

```python
import functools

import jax
import jax.numpy as jnp
from jax import lax
from jax.experimental import pallas as pl
from jax.experimental.pallas import tpu as pltpu
from jax.sharding import PartitionSpec as P

D = 6144
FF = 24576
PATCHES = 256
IMAGES = 4
SCALE = 1.0 / (float(D) * float(FF) * float(PATCHES)) ** 0.5
BF16 = jnp.bfloat16
F32 = jnp.float32


def gelu_terms(pre):
    cdf = 0.5 * (1.0 + lax.erf(pre * 0.7071067811865476))
    pdf = jnp.exp(-0.5 * pre * pre) * 0.3989422804014327
    return pre * cdf, cdf + pre * pdf


def sign_matrix(bits):
    return (2 * bits - 1).astype(BF16)


def members(patch_order):
    images = patch_order // PATCHES
    return (images[None, :] == jnp.arange(IMAGES, dtype=jnp.int32)[:, None]).astype(F32)


def gathered(normed, cotangent, w_up, w_down, sign_in_up, sign_out_up, sign_in_down, sign_out_down, patch_order):
    k = sign_in_up.shape[1]
    x = lax.all_gather(normed, "row", axis=0, tiled=True)
    g = lax.all_gather(cotangent, "row", axis=0, tiled=True)
    up = jnp.dot(x, w_up, preferred_element_type=F32)
    down = lax.dot_general(g, w_down, (((1,), (1,)), ((), ())), preferred_element_type=F32)
    proj = jnp.concatenate(
        [
            jnp.dot(x, sign_matrix(sign_in_up), preferred_element_type=F32),
            jnp.dot(g, sign_matrix(sign_out_down), preferred_element_type=F32),
        ],
        axis=1,
    )
    pre = lax.psum_scatter(up.astype(BF16), "col", scatter_dimension=1, tiled=True).astype(F32)
    back = lax.psum_scatter(down.astype(BF16), "col", scatter_dimension=1, tiled=True).astype(F32)
    proj = lax.psum(proj.astype(BF16), "col").astype(F32)
    units = pre.shape[1]
    first = lax.axis_index("col") * units
    sb = sign_matrix(lax.dynamic_slice_in_dim(sign_out_up, first, units, 0))
    sc = sign_matrix(lax.dynamic_slice_in_dim(sign_in_down, first, units, 0))
    act, slope = gelu_terms(pre)
    side_up = jnp.dot((back * slope).astype(BF16), sb, preferred_element_type=F32)
    side_down = jnp.dot(act.astype(BF16), sc, preferred_element_type=F32)
    table = members(patch_order)
    high = lax.Precision.HIGHEST
    up = jnp.einsum("it,tk,tl->ikl", table, proj[:, :k], side_up, precision=high)
    down = jnp.einsum("it,tk,tl->ikl", table, side_down, proj[:, k:], precision=high)
    return tuple(
        lax.psum_scatter(t.reshape(IMAGES, -1) * SCALE, ("row", "col"), scatter_dimension=1, tiled=True)
        for t in (up, down)
    )


def columns(w_ref, contract, j, tile):
    at = pl.ds(pl.multiple_of(j * tile, tile), tile)
    return w_ref.at[:, at] if contract == 0 else w_ref.at[at, :]


def partial_kernel(contract, tile, pick_ref, order_ref, *refs):
    n = 6 if contract == 0 else 2
    ins, w_ref, refs = refs[:n], refs[n], refs[n + 1 :]
    send_refs, (fwd_ref, keep_ref), refs = refs[:PIECES], refs[PIECES : PIECES + 2], refs[PIECES + 2 :]
    if contract == 0:
        rows, y_ref, w_v, row_sem, w_sem, out_sem, other, bits, other_sem, bits_sem = refs
    else:
        rows, y_ref, w_v, row_sem, w_sem, out_sem = refs
    tiles = w_ref.shape[1 - contract] // tile
    quarter = rows.shape[0] // 4
    firsts = [sum(SHARES[:n]) * quarter // 2 for n in range(PIECES)]
    parts = [(first, ref.shape[0], ref) for first, ref in zip(firsts, send_refs)]
    parts += [(2 * quarter, quarter, fwd_ref), (3 * quarter, quarter, keep_ref)]

    def row_copies(source, target, sem):
        return [
            pltpu.make_async_copy(
                source.at[pl.ds(pl.multiple_of(order_ref[j] * quarter, quarter), quarter), :],
                target.at[pl.ds(j * quarter, quarter), :],
                sem.at[j],
            )
            for j in range(4)
        ]

    for choice in (0, 1):

        @pl.when(pick_ref[0] == choice)
        def _():
            for copy in row_copies(ins[choice], rows, row_sem):
                copy.start()

    def load(j):
        return pltpu.make_async_copy(columns(w_ref, contract, j, tile), columns(w_v, contract, j, tile), w_sem.at[j])

    def puts(j, at):
        return [
            pltpu.make_async_copy(y_ref.at[pl.ds(first, count), at], out.at[:, at], out_sem.at[n, j])
            for n, (first, count, out) in enumerate(parts)
        ]

    def span(j):
        return pl.ds(pl.multiple_of(j * tile, tile), tile)

    for j in range(min(AHEAD, tiles)):
        load(j).start()
    for copy in row_copies(ins[0], rows, row_sem):
        copy.wait()
    if contract == 0:
        for choice in (0, 1):

            @pl.when(pick_ref[0] == choice)
            def _():
                for copy in row_copies(ins[2 + choice], other, other_sem):
                    copy.start()

        bit_copies = [pltpu.make_async_copy(ins[4 + n], bits.at[n], bits_sem.at[n]) for n in range(2)]
        for copy in bit_copies:
            copy.start()

    @pl.loop(0, tiles)
    def _(j):
        load(j).wait()

        @pl.when(j + AHEAD < tiles)
        def _():
            load(j + AHEAD).start()

        y_ref[:, span(j)] = lax.dot_general(
            rows[...],
            columns(w_v, contract, j, tile)[...],
            (((1,), (contract,)), ((), ())),
            preferred_element_type=F32,
        ).astype(BF16)
        for copy in puts(j, span(j)):
            copy.start()

    last = []
    if contract == 0:
        for copy in row_copies(ins[2], other, other_sem) + bit_copies:
            copy.wait()
        at = pl.ds(tiles * tile, 2 * bits.shape[1])
        y_ref[:, at] = jnp.concatenate(
            [
                lax.dot_general(
                    left[...], (2 * bits[n] - 1).astype(F32).astype(BF16), ACROSS_DIMS, preferred_element_type=F32
                )
                for n, left in enumerate((rows, other))
            ],
            axis=1,
        ).astype(BF16)
        last = puts(tiles, at)
        for copy in last:
            copy.start()

    @pl.loop(0, tiles)
    def _(j):
        for copy in puts(j, span(j)):
            copy.wait()

    for copy in last:
        copy.wait()


ACROSS_DIMS = (((1,), (1,)), ((), ()))
COST = 4.8e9
ECOST = 2.6e9
AHEAD = 3
SHARES = (1, 1, 2)
PIECES = len(SHARES)


def in_hbm(*arrays):
    return [pltpu.with_memory_space_constraint(a, pltpu.HBM) for a in arrays]


def partial_product(pick, order, x, w, contract, g=None, bits=None):
    tokens, depth = x[0].shape
    units = w.shape[1 - contract]
    tile = 1024 if units % 1024 == 0 else units
    tiles = units // tile
    quarter = tokens // 4
    anywhere = pl.BlockSpec(memory_space=pl.ANY)
    scalars = pl.BlockSpec(memory_space=pltpu.SMEM)
    ins, scratch, width = [*x], [], units
    if g is not None:
        ins += [*g, *bits]
        width += 2 * bits[0].shape[0]
        scratch = [
            pltpu.VMEM((tokens, depth), BF16),
            pltpu.VMEM((2, *bits[0].shape), bits[0].dtype),
            pltpu.SemaphoreType.DMA((4,)),
            pltpu.SemaphoreType.DMA((2,)),
        ]
    ins = in_hbm(*ins, w)
    return pl.pallas_call(
        functools.partial(partial_kernel, contract, tile),
        in_specs=[scalars, scalars] + [anywhere] * len(ins),
        out_specs=[anywhere] * (PIECES + 2),
        out_shape=[pltpu.HBM((share * quarter // 2, width), BF16) for share in SHARES]
        + [pltpu.VMEM((quarter, width), BF16), pltpu.HBM((quarter, width), BF16)],
        scratch_shapes=[
            pltpu.VMEM((tokens, depth), BF16),
            pltpu.VMEM((tokens, width), BF16),
            pltpu.VMEM(w.shape, BF16),
            pltpu.SemaphoreType.DMA((4,)),
            pltpu.SemaphoreType.DMA((tiles,)),
            pltpu.SemaphoreType.DMA((PIECES + 2, tiles + 1)),
        ]
        + scratch,
        compiler_params=pltpu.CompilerParams(vmem_limit_bytes=36 * 2**20),
        cost_estimate=pl.CostEstimate(flops=int(COST), bytes_accessed=1000, transcendentals=0),
    )(pick, order, *ins)


def add_kernel(a_ref, *refs):
    terms, (out_ref, slots, sems) = refs[:-3], refs[-3:]
    piece = terms[0].shape[0]
    copies = [pltpu.make_async_copy(a_ref, slots.at[0], sems.at[0])]
    for n, ref in enumerate(terms):
        copies.append(pltpu.make_async_copy(ref, slots.at[1, pl.ds(n * piece, piece), :], sems.at[1 + n]))
    for copy in copies:
        copy.start()
    for copy in copies:
        copy.wait()
    out_ref[...] = (slots[0].astype(F32) + slots[1].astype(F32)).astype(BF16)


def add_rows(a, b):
    return pl.pallas_call(
        add_kernel,
        in_specs=[pl.BlockSpec(memory_space=pl.ANY)] * (1 + len(b)),
        out_specs=pl.BlockSpec(memory_space=pltpu.VMEM),
        out_shape=jax.ShapeDtypeStruct(a.shape, BF16),
        scratch_shapes=[pltpu.VMEM((2, *a.shape), BF16), pltpu.SemaphoreType.DMA((1 + len(b),))],
        compiler_params=pltpu.CompilerParams(vmem_limit_bytes=16 * 2**20),
        cost_estimate=pl.CostEstimate(flops=1000, bytes_accessed=1000, transcendentals=0),
    )(pltpu.with_memory_space_constraint(a, pltpu.VMEM), *b)


def gathered_terms(refs, slots, sems):
    piece = refs[2].shape[0]
    copies = [
        pltpu.make_async_copy(refs[0], slots.at[0], sems.at[0]),
        pltpu.make_async_copy(refs[1], slots.at[1], sems.at[1]),
    ]
    for n, ref in enumerate(refs[2:]):
        copies.append(pltpu.make_async_copy(ref, slots.at[2, pl.ds(n * piece, piece), :], sems.at[2 + n]))
    for copy in copies:
        copy.start()
    return copies


def total(slots, at):
    return slots[0, :, at].astype(F32) + slots[1, :, at].astype(F32) + slots[2, :, at].astype(F32)


def over_chunks(units, body, init):
    chunk = 1024 if units % 1024 == 0 else units
    return lax.fori_loop(0, units // chunk, lambda j, c: body(pl.ds(pl.multiple_of(j * chunk, chunk), chunk), c), init)


def act_kernel(n, *refs):
    terms, (sc, down_ref, slope_ref, proj_ref, slots, sems) = refs[:n], refs[n:]
    for copy in gathered_terms(terms, slots, sems):
        copy.wait()
    units = slope_ref.shape[1]

    def body(at, side):
        act, slope = gelu_terms(total(slots, at))
        slope_ref[:, at] = slope
        return side + lax.dot_general(act.astype(BF16), sc[:, at], ACROSS_DIMS, preferred_element_type=F32)

    down_ref[...] = over_chunks(units, body, jnp.zeros(down_ref.shape, F32))
    proj_ref[...] = total(slots, pl.ds(units, proj_ref.shape[1]))


def back_kernel(n, *refs):
    terms, (slope_ref, sb, up_ref, slots, sems) = refs[:n], refs[n:]
    for copy in gathered_terms(terms, slots, sems):
        copy.wait()

    def body(at, side):
        dpre = (total(slots, at) * slope_ref[:, at]).astype(BF16)
        return side + lax.dot_general(dpre, sb[:, at], ACROSS_DIMS, preferred_element_type=F32)

    up_ref[...] = over_chunks(slope_ref.shape[1], body, jnp.zeros(up_ref.shape, F32))


def sides_kernel(n, steps, *refs):
    terms = refs[: 2 * n * steps]
    b_ref, c_ref, up_ref, down_ref, proj_ref, sb, sc, ups, downs, bits, sems, bit_sems = refs[2 * n * steps :]
    quarter, units = downs.shape[2:]
    bit_copies = [
        pltpu.make_async_copy(b_ref, bits.at[0], bit_sems.at[0]),
        pltpu.make_async_copy(c_ref, bits.at[1], bit_sems.at[1]),
    ]
    for copy in bit_copies:
        copy.start()

    def fetch(s):
        up, down = terms[2 * n * s : 2 * n * s + n], terms[2 * n * s + n : 2 * n * s + 2 * n]
        return gathered_terms(up, ups.at[s % 2], sems.at[s, 0]) + gathered_terms(down, downs.at[s % 2], sems.at[s, 1])

    coming = fetch(0)
    for copy in bit_copies:
        copy.wait()
    sb[...] = (2 * bits[0] - 1).astype(F32).astype(BF16)
    sc[...] = (2 * bits[1] - 1).astype(F32).astype(BF16)
    for s in range(steps):
        for copy in coming:
            copy.wait()
        if s + 1 < steps:
            coming = fetch(s + 1)

        def body(at, both):
            act, slope = gelu_terms(total(ups.at[s % 2], at))
            dpre = (total(downs.at[s % 2], at) * slope).astype(BF16)
            return (
                both[0] + lax.dot_general(dpre, sb[:, at], ACROSS_DIMS, preferred_element_type=F32),
                both[1] + lax.dot_general(act.astype(BF16), sc[:, at], ACROSS_DIMS, preferred_element_type=F32),
            )

        zeros = jnp.zeros((quarter, up_ref.shape[1]), F32)
        side_up, side_down = over_chunks(units, body, (zeros, zeros))
        mine = slice(s * quarter, (s + 1) * quarter)
        up_ref[mine] = side_up
        down_ref[mine] = side_down
        proj_ref[mine] = total(ups.at[s % 2], pl.ds(units, proj_ref.shape[1]))


def side_call(kernel, terms, others, outs, scratch, cost):
    vmem, anywhere = pl.BlockSpec(memory_space=pltpu.VMEM), pl.BlockSpec(memory_space=pl.ANY)
    others, in_vmem = zip(*others)
    return pl.pallas_call(
        kernel,
        in_specs=[anywhere] * len(terms) + [vmem if v else anywhere for v in in_vmem],
        out_specs=[vmem] * len(outs),
        out_shape=outs,
        scratch_shapes=scratch,
        compiler_params=pltpu.CompilerParams(vmem_limit_bytes=24 * 2**20),
        cost_estimate=pl.CostEstimate(flops=int(cost), bytes_accessed=1000, transcendentals=0),
    )(*in_hbm(*terms), *others)


SIBLING = [(0, 1), (1, 0), (2, 3), (3, 2)]
ACROSS = [(0, 2), (2, 0), (1, 3), (3, 1)]


def pipelined(normed, cotangent, w_up, w_down, sign_in_up, sign_out_up, sign_in_down, sign_out_down, patch_order):
    k = sign_in_up.shape[1]
    col = lax.axis_index("col")
    row = lax.axis_index("row")
    shard = normed.shape[0]
    quarter = shard // 4
    order = jnp.stack([3 - col, col ^ 1, col ^ 2, col]).astype(jnp.int32)
    inner = (row == 1) | (row == 2)

    def hop(a, pairs):
        return lax.ppermute(a, "row", pairs)

    def tie(a, *others):
        return lax.optimization_barrier((a, *others))[0]

    zero = jnp.zeros((1,), jnp.int32)
    pick = jnp.where(inner, 0, 1).astype(jnp.int32).reshape(1)
    PAIRS, MIDDLE, OUTER = [(0, 1), (1, 0), (2, 3), (3, 2)], [(1, 2), (2, 1)], [(1, 0), (2, 3)]
    sources = [row, row ^ 1, jnp.where(row < 2, 2, 1), jnp.where(row < 2, 3, 0)]
    weights = (w_up, w_down)
    bits = (sign_in_up.T, sign_out_down.T)
    shards = [normed, cotangent]
    products, received, outs, far = [], [], [], []

    def product(i, p, x, g, *after):
        if after:
            p = tie(p, *after)
        extra = (g, bits) if i % 2 == 0 else ()
        products.append(partial_product(p, order, g if i % 2 else x, weights[i % 2], i % 2, *extra))
        received.append([lax.ppermute(send, "col", SIBLING) for send in products[i][:PIECES]])

    def combine(i, after=None):
        got = received[i]
        if after is not None:
            got = tie(got, after)
        outs.append((add_rows(products[i][PIECES], got[:-1]), got[-1:]))
        far.append(lax.ppermute(outs[i][0], "col", ACROSS))

    def terms(i):
        return (products[i][PIECES + 1], far[i], *outs[i][1])

    x, g = shards
    x1, x2 = hop(x, PAIRS), hop(x, MIDDLE)
    product(0, zero, (x, x), (g, g))
    combine(0)
    product(1, zero, (x, x), (g, g), outs[0][0], x1, x2)
    g1, g2 = hop(g, PAIRS), hop(g, MIDDLE)
    combine(1)
    product(2, zero, (x1, x1), (g1, g1), outs[1][0], far[0], g1, g2)
    x2b, x3 = hop(x2, OUTER), hop(tie(x1, products[1][0]), MIDDLE)
    combine(2)
    product(3, zero, (x1, x1), (g1, g1), outs[2][0], far[1], x2b, x3)
    g2b, g3 = hop(g2, OUTER), hop(tie(g1, products[2][0]), MIDDLE)
    combine(3)
    product(4, pick, (x2, x2b), (g2, g2b), outs[3][0], far[2], g2b, g3)
    x3b = hop(tie(x3, products[3][0]), OUTER)
    combine(4)
    product(5, pick, (x2, x2b), (g2, g2b), outs[4][0], far[3], x3b)
    g3b = hop(tie(g3, products[4][0]), OUTER)
    combine(5)
    product(6, pick, (x3, x3b), (g3, g3b), outs[5][0], far[4], g3b)
    combine(6)
    product(7, pick, (x3, x3b), (g3, g3b), outs[6][0], far[5])
    combine(7, far[6])
    n, units = len(terms(0)), w_up.shape[1]
    b, c = tie((sign_out_up, sign_in_down), outs[7][0])
    early = 3 * quarter
    sides_up, sides_down, projs, sb, sc = side_call(
        functools.partial(sides_kernel, n, 3),
        [t for i in range(6) for t in terms(i)],
        [(b.T, False), (c.T, False)],
        [jax.ShapeDtypeStruct((early, k), F32)] * 2
        + [jax.ShapeDtypeStruct((early, 2 * k), F32)]
        + [jax.ShapeDtypeStruct((k, units), BF16)] * 2,
        [
            pltpu.VMEM((2, 3, quarter, units + 2 * k), BF16),
            pltpu.VMEM((2, 3, quarter, units), BF16),
            pltpu.VMEM((2, k, units), jnp.int32),
            pltpu.SemaphoreType.DMA((3, 2, n)),
            pltpu.SemaphoreType.DMA((2,)),
        ],
        1000,
    )
    down, slope, last = side_call(
        functools.partial(act_kernel, n),
        terms(6),
        [(sc, True)],
        [
            jax.ShapeDtypeStruct((quarter, k), F32),
            jax.ShapeDtypeStruct((quarter, units), F32),
            jax.ShapeDtypeStruct((quarter, 2 * k), F32),
        ],
        [pltpu.VMEM((3, quarter, units + 2 * k), BF16), pltpu.SemaphoreType.DMA((n,))],
        ECOST,
    )
    up = side_call(
        functools.partial(back_kernel, n),
        terms(7),
        [(slope, True), (sb, True)],
        [jax.ShapeDtypeStruct((quarter, k), F32)],
        [pltpu.VMEM((3, quarter, units), BF16), pltpu.SemaphoreType.DMA((n,))],
        1000,
    )[0]
    side_up = jnp.concatenate([sides_up, up])
    side_down = jnp.concatenate([sides_down, down])
    proj = jnp.concatenate([projs, last])

    table = members(patch_order)
    tables = [
        lax.dynamic_slice_in_dim(table, sources[s] * shard + col * quarter, quarter, 1) for s in range(4)
    ]
    table = jnp.concatenate(tables, axis=1)
    high = lax.Precision.HIGHEST
    up = jnp.einsum("it,tk,tl->ikl", table, proj[:, :k], side_up, precision=high)
    down = jnp.einsum("it,tk,tl->ikl", table, side_down, proj[:, k:], precision=high)
    both = jnp.stack([up.reshape(IMAGES, 4, 4, -1), down.reshape(IMAGES, 4, 4, -1)]) * SCALE
    both = both.transpose(2, 3, 0, 1, 4)

    both = both.reshape(4, 2, 2, *both.shape[2:])
    chip, core = col // 2, col % 2
    mine = lax.dynamic_index_in_dim(both, chip, 1, keepdims=False)
    theirs = lax.dynamic_index_in_dim(both, 1 - chip, 1, keepdims=False)
    both = mine + lax.ppermute(theirs, "col", ACROSS)
    mine = lax.dynamic_index_in_dim(both, core, 1, keepdims=False)
    theirs = lax.dynamic_index_in_dim(both, 1 - core, 1, keepdims=False)
    both = mine + lax.ppermute(theirs, "col", SIBLING)
    total = lax.dynamic_index_in_dim(both, row, 0, keepdims=False)
    for off in (1, 2, 3):
        block = lax.dynamic_index_in_dim(both, row ^ off, 0, keepdims=False)
        total = total + hop(block, [(i, i ^ off) for i in range(4)])
    return total[0], total[1]


def solution(mesh):
    line = mesh.shape["row"] == 4 and mesh.shape["col"] == 4
    in_specs = (
        P(("parts", "row"), "col"),
        P(("parts", "row"), "col"),
        P("col", "row"),
        P("row", "col"),
        P("col", None),
        P("row", None),
        P("row", None),
        P("col", None),
        P("parts"),
    )
    out_specs = (P("parts", ("row", "col")), P("parts", ("row", "col")))
    return jax.shard_map(
        pipelined if line else gathered, mesh=mesh, in_specs=in_specs, out_specs=out_specs, check_vma=False
    )
```
